32 devices in a mesh: groups: 2 (over x), row: 16 (over z, y, core).
Axes of the slice: x: 2, y: 2, z: 4, core: 2. Of those that a mesh axis runs over, the one named last changes fastest.
Arguments:
- partner_aux_tiles: bfloat16 [256, 64, 1024], P(('groups', 'row')), parts along dimension 0, may hold values from -0.1875 to 0.1875
- row_aux_tiles: bfloat16 [256, 64, 1024], P(('groups', 'row')), parts along dimension 0, may hold values from -6 to 6
- tile_partner: int32 [256], P(('groups', 'row')), parts along dimension 0, may hold values from 0 to 15, as said below
- tile_count: int32 [32], P(('groups', 'row')), parts along dimension 0, may hold values from 1 to 8
- density_blocks: bfloat16 [256, 64, 64], P(('groups', 'row')), parts along dimension 0, may hold values from -0.25 to 0.25
- density_cols: int32 [256], P(('groups', 'row')), parts along dimension 0, may hold values from 0 to 15, as said below
- density_count: int32 [32], P(('groups', 'row')), parts along dimension 0, may hold values from 1 to 8
Outputs:
- exchange_window: float32 [2048, 704], P(('groups', 'row')), parts along dimension 0
The draws below stay inside these ranges and needn't reach their ends.
There are 2 independent parts, one for each index of `groups`. The reference program is written for one: setup_inputs(seed, part) draws one part's arguments, and reference() takes and returns one part's arrays. A program takes and returns all parts, laid end to end along the dimension named above; each array names one. Nothing has to cross between parts.
Inputs may be any that keep to these rules, and one draw needn't show every extreme that they name: `tile_partner`: the 8 slots of one row block name distinct atom blocks within 5 blocks of it along the periodic order of 16 blocks. `density_cols`: the 8 slots of one row block name distinct atom blocks within 5 blocks of it along the periodic order of 16 blocks.
All inputs are finite; a program needn't handle non-finite values.
Results may differ from the reference program's by a relative error of at most 0.0029.
Values may be sent and summed in bfloat16 or wider, within the bound.
A program may use at most 64 MiB of HBM per device.

```python
import jax
import jax.numpy as jnp
from jax import lax

BLK = 64
AUX_BLK = 16
REACH = 5
NT = 8
ND = 8
NBLK = 16


def neighbour_blocks(key, slots):
    keys = jax.random.split(key, NBLK)
    orders = jax.vmap(lambda one_key: jax.random.permutation(one_key, 2 * REACH + 1))(keys)
    row_ids = jnp.arange(NBLK, dtype=jnp.int32)[:, None]
    chosen = orders[:, :slots].astype(jnp.int32) - REACH
    return ((row_ids + chosen) % NBLK).reshape(-1).astype(jnp.int32)


def ragged_counts(key, most):
    counts = jax.random.randint(key, (NBLK,), 1, most + 1)
    fullest = jax.random.randint(jax.random.fold_in(key, 1), (), 0, NBLK)
    return jnp.where(jnp.arange(NBLK) == fullest, most, counts).astype(jnp.int32)


def draw_tile_partner(key, part):
    key = jax.random.fold_in(key, 11)
    return neighbour_blocks(key, NT)


def draw_tile_count(key, part):
    key = jax.random.fold_in(key, 12)
    return ragged_counts(key, NT)


def draw_density_cols(key, part):
    key = jax.random.fold_in(key, 13)
    return neighbour_blocks(key, ND)


def draw_density_count(key, part):
    key = jax.random.fold_in(key, 14)
    return ragged_counts(key, ND)


def level_of(rng, shape, cuts, least, top_value):
    level, own = 1.0, jax.random.fold_in(rng, 6)
    for axis_at, shards_of in cuts:
        steps = jnp.exp(jax.random.uniform(jax.random.fold_in(own, axis_at), (shards_of,), jnp.float32, least / len(cuts), top_value / len(cuts)))
        level = level * jnp.repeat(steps, shape[axis_at] // shards_of).reshape([-1 if axis == axis_at else 1 for axis in range(len(shape))])
    return level


def noise(key, shape, deviation, reach, cuts=(), kind=jnp.bfloat16):
    loudness = level_of(key, shape, cuts, -0.22, 0.18) if cuts else 1.0
    entries = jax.random.normal(key, shape, jnp.float32) * deviation * loudness
    return jnp.minimum(jnp.maximum(entries, -reach), reach).astype(kind)


def setup_inputs(seed: int = 0, part: int = 0) -> dict:
    key_list = jax.random.split(jax.random.key(seed), 8)
    own_keys = jax.random.split(jax.random.fold_in(key_list[7], part), 8)
    return {
        "partner_aux_tiles": noise(own_keys[0], (NBLK * NT, BLK, BLK * AUX_BLK), (BLK * AUX_BLK) ** -0.5, 0.1875, ((0, 16),)),
        "row_aux_tiles": noise(own_keys[1], (NBLK * NT, BLK, BLK * AUX_BLK), 1.0, 6.0, ((0, 16),)),
        "tile_partner": draw_tile_partner(jax.random.fold_in(jax.random.fold_in(key_list[7], part), 71), part),
        "tile_count": draw_tile_count(jax.random.fold_in(jax.random.fold_in(key_list[7], part), 71), part),
        "density_blocks": noise(own_keys[4], (NBLK * ND, BLK, BLK), (NT * BLK) ** -0.5, 0.25, ((0, 16),)),
        "density_cols": draw_density_cols(jax.random.fold_in(jax.random.fold_in(key_list[7], part), 71), part),
        "density_count": draw_density_count(jax.random.fold_in(jax.random.fold_in(key_list[7], part), 71), part),
    }


def reference(partner_aux_tiles, row_aux_tiles, tile_partner, tile_count, density_blocks, density_cols, density_count):
    window = 2 * REACH + 1
    row_ids = jnp.arange(NBLK, dtype=jnp.int32)
    partner = tile_partner.reshape(NBLK, NT)
    active = jnp.arange(NT, dtype=jnp.int32)[None, :] < tile_count[:, None]
    dense_cols = density_cols.reshape(NBLK, ND)
    dense_on = jnp.arange(ND, dtype=jnp.int32)[None, :] < density_count[:, None]
    offsets = (partner - row_ids[:, None] + REACH) % NBLK - REACH
    row_tiles = row_aux_tiles.reshape(NBLK, NT, BLK, BLK, AUX_BLK)
    pair_tiles = partner_aux_tiles.reshape(NBLK, NT, BLK, BLK * AUX_BLK)
    density = density_blocks.reshape(NBLK, ND, BLK, BLK)

    def contract(pieces):
        tiles_r, partner_r, active_r, density_r, cols_r, dense_r = pieces
        matches = (partner_r[:, None] == cols_r[None, :]) & active_r[:, None] & dense_r[None, :]
        selected = jnp.einsum('uj,jac->uac', matches.astype(jnp.float32), density_r.astype(jnp.float32)).astype(jnp.bfloat16)
        result = jnp.einsum('uac,ukcp->kap', selected.astype(jnp.float32), tiles_r.astype(jnp.float32))
        return result.reshape(BLK, BLK * AUX_BLK).astype(jnp.bfloat16)

    contracted = lax.map(contract, (row_tiles, partner, active, density, dense_cols, dense_on))
    relative = jnp.arange(window, dtype=jnp.int32) - REACH

    def project(pieces):
        tiles_r, offsets_r, active_r, row_now = pieces
        picked = (offsets_r[:, None] == relative[None, :]) & active_r[:, None]
        chosen = jnp.einsum('ts,tix->six', picked.astype(jnp.float32), tiles_r.astype(jnp.float32)).astype(jnp.bfloat16)
        nearby = jnp.take(contracted, ((row_now + relative) % NBLK).astype(jnp.int32), axis=0)
        return jnp.einsum('six,skx->isk', chosen.astype(jnp.float32), nearby.astype(jnp.float32))

    half_term = lax.map(project, (pair_tiles, offsets, active, row_ids))
    columns = []
    for column in range(window):
        offset_now = column - REACH
        mirrored = jnp.roll(half_term[:, :, window - 1 - column, :], -offset_now, axis=0)
        columns.append(half_term[:, :, column, :] + jnp.swapaxes(mirrored, 1, 2))
    return jnp.stack(columns, axis=2).reshape(NBLK * BLK, window * BLK)
```

```python
import functools

import jax
import jax.numpy as jnp
from jax import lax
from jax.experimental import pallas as pl
from jax.experimental.pallas import tpu as pltpu
from jax.sharding import PartitionSpec as P

REACH = 5
CHUNKS = 2
DIRECT = (2, -2, 4, -4)
N_T = (((1,), (1,)), ((), ()))


def kernel(n, row_hbm, pair_hbm, partner, count, density, cols, dense_count, out,
           row_v, pair_v, perm, row_p, pair_p, weights, mine, near, half, leaving, mirror,
           load_sem, send_sem, pass_sem, near_sem, back_sem, mirror_sem):
    slots, blk, width = row_v.shape
    dense = density.shape[0]
    aux = width // blk
    group = 256
    n_group = width // group
    per_chunk = n_group // CHUNKS
    span = width // CHUNKS

    me = lax.axis_index("row")
    core = lax.rem(me, 2)
    side = 1 - 2 * core

    def at(offset):
        return {"row": lax.rem(me + offset + n, n)}

    load_row = pltpu.make_async_copy(row_hbm, row_v, load_sem.at[0])
    load_pair = pltpu.make_async_copy(pair_hbm, pair_v, load_sem.at[1])
    load_row.start()
    load_pair.start()
    barrier = pltpu.get_barrier_semaphore()
    for offset in range(-REACH, REACH + 1):
        if offset:
            pl.semaphore_signal(barrier, inc=1, device_id=at(offset),
                                device_id_type=pl.DeviceIdType.MESH)

    x = lax.broadcasted_iota(jnp.int32, (width, 128), 0)
    goes_to = lax.div(x, aux) + lax.rem(x, aux) * blk
    lane = lax.broadcasted_iota(jnp.int32, (width, 128), 1)
    for tile in range(width // 128):
        perm[:, tile * 128:(tile + 1) * 128] = jnp.where(
            goes_to == lane + tile * 128, 1.0, 0.0).astype(jnp.bfloat16)

    live_tiles = count[0]
    live_dense = dense_count[0]
    zero = jnp.zeros((blk, blk), jnp.bfloat16)
    wide_zero = jnp.zeros((2 * blk, 2 * blk), jnp.bfloat16)
    for u in range(slots):
        index = jnp.int32(0)
        found = jnp.int32(0)
        for j in range(dense):
            hit = ((cols[j] == partner[u]) & (j < live_dense)).astype(jnp.int32)
            index += hit * j
            found += hit
        found *= (u < live_tiles).astype(jnp.int32)
        d = (density[index].astype(jnp.float32) * found.astype(jnp.float32)).astype(jnp.bfloat16)
        left = jnp.concatenate([d, zero], axis=1)
        right = jnp.concatenate([zero, d], axis=1)
        weights[u, 0:64, 0:128] = left
        weights[u, 64:128, 0:128] = right
        weights[u, 128:192, 128:256] = left
        weights[u, 192:256, 128:256] = right
        weights[u, 0:128, 128:256] = wide_zero
        weights[u, 128:256, 0:128] = wide_zero

    def reorder(source, target, g):
        flat = source[...].reshape(slots * blk, width)
        part = jnp.dot(flat, perm[:, g * group:(g + 1) * group],
                       preferred_element_type=jnp.float32)
        target[:, :, g * group:(g + 1) * group] = part.astype(jnp.bfloat16).reshape(
            slots, blk, group)

    sends = []
    load_row.wait()
    for h in range(CHUNKS):
        for step in range(per_chunk):
            g = h * per_chunk + step
            reorder(row_v, row_p, g)
            total = jnp.zeros((blk, group), jnp.float32)
            for u in range(slots):
                total += lax.dot_general(row_p[u, :, g * group:(g + 1) * group], weights[u], N_T,
                                         preferred_element_type=jnp.float32)
            mine[h, :, step * group:(step + 1) * group] = total.astype(jnp.bfloat16)
        if h == 0:
            pl.semaphore_wait(barrier, 2 * REACH)
        for slot, offset in ((0, -2), (1, 2), (2, -4), (3, 4), (4, side), (9, -5 * side)):
            number = slot if slot < 5 else 5
            copy = pltpu.make_async_remote_copy(
                src_ref=mine.at[h], dst_ref=near.at[slot, h],
                send_sem=send_sem.at[number, h], recv_sem=near_sem.at[slot, h],
                device_id=at(offset), device_id_type=pl.DeviceIdType.MESH)
            copy.start()
            sends.append(copy)

    def arrived(slot, h):
        pltpu.make_async_remote_copy(
            src_ref=mine.at[h], dst_ref=near.at[slot, h],
            send_sem=send_sem.at[0, h], recv_sem=near_sem.at[slot, h],
            device_id=at(side), device_id_type=pl.DeviceIdType.MESH).wait_recv()

    load_pair.wait()
    for g in range(n_group):
        reorder(pair_v, pair_p, g)

    where = [lax.rem(partner[t] - me + REACH + n, n) - REACH for t in range(slots)]

    def term(offset, block):
        index = jnp.int32(0)
        found = jnp.int32(0)
        for t in range(slots):
            hit = ((where[t] == offset) & (t < live_tiles)).astype(jnp.int32)
            index += hit * t
            found += hit
        total = jnp.zeros((blk, blk), jnp.float32)
        for h in range(CHUNKS):
            total += lax.dot_general(pair_p[index, :, h * span:(h + 1) * span], block(h), N_T,
                                     preferred_element_type=jnp.float32)
        return total * found.astype(jnp.float32)

    own = term(0, lambda h: mine[h])
    half[REACH] = own + own.T

    for h in range(CHUNKS):
        for slot in range(4):
            arrived(slot, h)
            copy = pltpu.make_async_remote_copy(
                src_ref=near.at[slot, h], dst_ref=near.at[5 + slot, h],
                send_sem=pass_sem.at[slot, h], recv_sem=near_sem.at[5 + slot, h],
                device_id=at(side), device_id_type=pl.DeviceIdType.MESH)
            copy.start()
            sends.append(copy)

    order = [(4, side), (0, 2), (1, -2), (5, 2 + side), (6, -2 + side), (2, 4), (3, -4),
             (7, 4 + side), (8, -4 + side), (9, -5 * side)]
    for slot, offset in order:
        if slot >= 4:
            for h in range(CHUNKS):
                arrived(slot, h)
        value = term(offset, lambda h: near[slot, h])
        half[REACH + offset] = value
        turned = value.T
        leaving[slot] = jnp.concatenate([turned[:blk // 2], turned[blk // 2:]], axis=1)
        copy = pltpu.make_async_remote_copy(
            src_ref=leaving.at[slot], dst_ref=mirror.at[REACH - offset],
            send_sem=back_sem.at[slot], recv_sem=mirror_sem.at[REACH - offset],
            device_id=at(offset), device_id_type=pl.DeviceIdType.MESH)
        copy.start()
        sends.append(copy)

    for s in range(2 * REACH + 1):
        value = half[s]
        if s != REACH:
            pltpu.make_async_remote_copy(
                src_ref=leaving.at[0], dst_ref=mirror.at[s],
                send_sem=back_sem.at[0], recv_sem=mirror_sem.at[s],
                device_id=at(side), device_id_type=pl.DeviceIdType.MESH).wait_recv()
            other = mirror[s]
            value += jnp.concatenate([other[:, :blk], other[:, blk:]], axis=0)
        out[:, s * blk:(s + 1) * blk] = value
    for copy in sends:
        copy.wait_send()


def body(partner_aux_tiles, row_aux_tiles, tile_partner, tile_count, density_blocks,
         density_cols, density_count):
    n = lax.axis_size("row")
    slots, blk, width = row_aux_tiles.shape
    window = 2 * REACH + 1
    span = width // CHUNKS
    vmem = pl.BlockSpec(memory_space=pltpu.VMEM)
    smem = pl.BlockSpec(memory_space=pltpu.SMEM)
    hbm = pl.BlockSpec(memory_space=pl.ANY)
    bf16 = jnp.bfloat16
    return pl.pallas_call(
        functools.partial(kernel, n),
        out_shape=jax.ShapeDtypeStruct((blk, window * blk), jnp.float32),
        in_specs=[hbm, hbm, smem, smem, vmem, smem, smem],
        out_specs=vmem,
        scratch_shapes=[
            pltpu.VMEM((slots, blk, width), bf16),
            pltpu.VMEM((slots, blk, width), bf16),
            pltpu.VMEM((width, width), bf16),
            pltpu.VMEM((slots, blk, width), bf16),
            pltpu.VMEM((slots, blk, width), bf16),
            pltpu.VMEM((slots, 256, 256), bf16),
            pltpu.VMEM((CHUNKS, blk, span), bf16),
            pltpu.VMEM((10, CHUNKS, blk, span), bf16),
            pltpu.VMEM((window, blk, blk), jnp.float32),
            pltpu.VMEM((10, blk // 2, 2 * blk), jnp.float32),
            pltpu.VMEM((window, blk // 2, 2 * blk), jnp.float32),
            pltpu.SemaphoreType.DMA((2,)),
            pltpu.SemaphoreType.DMA((6, CHUNKS)),
            pltpu.SemaphoreType.DMA((4, CHUNKS)),
            pltpu.SemaphoreType.DMA((10, CHUNKS)),
            pltpu.SemaphoreType.DMA((10,)),
            pltpu.SemaphoreType.DMA((window,)),
        ],
        compiler_params=pltpu.CompilerParams(
            collective_id=0, has_side_effects=True, vmem_limit_bytes=40 * 2**20),
        cost_estimate=pl.CostEstimate(flops=2 * 10**9, bytes_accessed=3 * 2**20, transcendentals=0),
    )(row_aux_tiles, partner_aux_tiles, tile_partner, tile_count, density_blocks, density_cols,
      density_count)


def solution(mesh):
    in_specs = (
        P(("groups", "row"), None, None),
        P(("groups", "row"), None, None),
        P(("groups", "row")),
        P(("groups", "row")),
        P(("groups", "row"), None, None),
        P(("groups", "row")),
        P(("groups", "row")),
    )
    out_specs = P(("groups", "row"), None)
    return jax.shard_map(body, mesh=mesh, in_specs=in_specs, out_specs=out_specs, check_vma=False)
```

```python
import functools

import jax
import jax.numpy as jnp
from jax import lax
from jax.experimental import pallas as pl
from jax.experimental.pallas import tpu as pltpu
from jax.sharding import PartitionSpec as P

REACH = 5
CHUNKS = 4
N_T = (((1,), (1,)), ((), ()))


def kernel(n, row_hbm, pair_hbm, partner, count, density_hbm, cols, dense_count, out,
           row_v, pair_v, density, perm, row_p, pair_p, weights, mine, near, half, leaving, mirror,
           load_sem, send_sem, pass_sem, near_sem, back_sem, mirror_sem):
    slots, blk, width = row_v.shape
    dense = density.shape[0]
    aux = width // blk
    group = 256
    n_group = width // group
    per_chunk = n_group // CHUNKS
    span = width // CHUNKS

    me = lax.axis_index("row")
    core = lax.rem(me, 2)
    column = lax.rem(lax.div(me, 2), 2)
    side = 1 - 2 * core
    ahead = 1 - 2 * column
    inner = lax.rem(core + column, 2)

    def at(offset):
        return {"row": lax.rem(me + offset + n, n)}

    load_row = pltpu.make_async_copy(row_hbm, row_v, load_sem.at[0])
    load_pair = pltpu.make_async_copy(pair_hbm, pair_v, load_sem.at[1])
    load_density = pltpu.make_async_copy(density_hbm, density, load_sem.at[2])
    load_density.start()
    load_row.start()
    load_pair.start()
    barrier = pltpu.get_barrier_semaphore()
    for offset in range(-REACH, REACH + 1):
        if offset:
            pl.semaphore_signal(barrier, inc=1, device_id=at(offset),
                                device_id_type=pl.DeviceIdType.MESH)

    x = lax.broadcasted_iota(jnp.int32, (width, 128), 0)
    goes_to = lax.div(x, aux) + lax.rem(x, aux) * blk
    lane = lax.broadcasted_iota(jnp.int32, (width, 128), 1)
    for tile in range(width // 128):
        perm[:, tile * 128:(tile + 1) * 128] = jnp.where(
            goes_to == lane + tile * 128, 1.0, 0.0).astype(jnp.bfloat16)

    load_density.wait()
    live_tiles = count[0]
    live_dense = dense_count[0]
    zero = jnp.zeros((blk, blk), jnp.bfloat16)
    wide_zero = jnp.zeros((2 * blk, 2 * blk), jnp.bfloat16)
    for u in range(slots):
        index = jnp.int32(0)
        found = jnp.int32(0)
        for j in range(dense):
            hit = ((cols[j] == partner[u]) & (j < live_dense)).astype(jnp.int32)
            index += hit * j
            found += hit
        found *= (u < live_tiles).astype(jnp.int32)
        d = (density[index].astype(jnp.float32) * found.astype(jnp.float32)).astype(jnp.bfloat16)
        left = jnp.concatenate([d, zero], axis=1)
        right = jnp.concatenate([zero, d], axis=1)
        weights[u, 0:64, 0:128] = left
        weights[u, 64:128, 0:128] = right
        weights[u, 128:192, 128:256] = left
        weights[u, 192:256, 128:256] = right
        weights[u, 0:128, 128:256] = wide_zero
        weights[u, 128:256, 0:128] = wide_zero

    def reorder(source, target, g):
        flat = source[...].reshape(slots * blk, width)
        part = jnp.dot(flat, perm[:, g * group:(g + 1) * group],
                       preferred_element_type=jnp.float32)
        target[:, :, g * group:(g + 1) * group] = part.astype(jnp.bfloat16).reshape(
            slots, blk, group)

    sends = []

    def to_slot(source, slot, h, sem, offset):
        return pltpu.make_async_remote_copy(
            src_ref=source, dst_ref=near.at[slot, h], send_sem=sem, recv_sem=near_sem.at[slot, h],
            device_id=at(offset), device_id_type=pl.DeviceIdType.MESH)

    def put(source, slot, h, sem, offset):
        copy = to_slot(source, slot, h, sem, offset)
        copy.start()
        sends.append(copy)

    load_row.wait()
    for h in range(CHUNKS):
        for step in range(per_chunk):
            g = h * per_chunk + step
            reorder(row_v, row_p, g)
            total = jnp.zeros((blk, group), jnp.float32)
            for u in range(slots):
                total += lax.dot_general(row_p[u, :, g * group:(g + 1) * group], weights[u], N_T,
                                         preferred_element_type=jnp.float32)
            mine[h, :, step * group:(step + 1) * group] = total.astype(jnp.bfloat16)
        if h == 0:
            pl.semaphore_wait(barrier, 2 * REACH)
        for number, slot, offset in ((0, 1, -4 * ahead), (1, 2, 4 * ahead), (2, 0, 2 * ahead),
                                     (3, 4, side)):
            put(mine.at[h], slot, h, send_sem.at[number, h], offset)
        far = to_slot(mine.at[h], 9, h, send_sem.at[4, h], -5 * ahead)

        @pl.when(inner == 0)
        def _():
            far.start()

        sends.append(far)

    def arrived(slot, h):
        to_slot(mine.at[h], slot, h, send_sem.at[0, h], side).wait_recv()

    def pass_on(h):
        for slot in (1, 2, 0, 3):
            arrived(slot, h)
            if slot == 1:
                put(near.at[1, h], 3, h, pass_sem.at[4, h], 2 * ahead)
            if slot == 2:
                @pl.when(inner == 1)
                def _():
                    to_slot(near.at[2, h], 9, h, send_sem.at[4, h], ahead).start()
            put(near.at[slot, h], 5 + slot, h, pass_sem.at[slot, h], side)

    load_pair.wait()
    for g in range(n_group):
        reorder(pair_v, pair_p, g)
        pass_on(g)

    where = [lax.rem(partner[t] - me + REACH + n, n) - REACH for t in range(slots)]

    def term(offset, block):
        index = jnp.int32(0)
        found = jnp.int32(0)
        for t in range(slots):
            hit = ((where[t] == offset) & (t < live_tiles)).astype(jnp.int32)
            index += hit * t
            found += hit
        total = jnp.zeros((blk, blk), jnp.float32)
        for h in range(CHUNKS):
            total += lax.dot_general(pair_p[index, :, h * span:(h + 1) * span], block(h), N_T,
                                     preferred_element_type=jnp.float32)
        return total * found.astype(jnp.float32)

    own = term(0, lambda h: mine[h])
    half[REACH] = own + own.T

    order = [(4, side), (0, 2 * ahead), (1, 4 * ahead), (2, -4 * ahead), (3, -2 * ahead),
             (5, side + 2 * ahead), (6, side + 4 * ahead), (7, side - 4 * ahead),
             (8, side - 2 * ahead), (9, -5 * side)]
    for slot, offset in order:
        if slot >= 4:
            for h in range(CHUNKS):
                arrived(slot, h)
        value = term(offset, lambda h: near[slot, h])
        half[REACH + offset] = value
        turned = value.T
        leaving[slot] = jnp.concatenate([turned[:blk // 2], turned[blk // 2:]], axis=1)
        copy = pltpu.make_async_remote_copy(
            src_ref=leaving.at[slot], dst_ref=mirror.at[REACH - offset],
            send_sem=back_sem.at[slot], recv_sem=mirror_sem.at[REACH - offset],
            device_id=at(offset), device_id_type=pl.DeviceIdType.MESH)
        copy.start()
        sends.append(copy)

    for s in range(2 * REACH + 1):
        value = half[s]
        if s != REACH:
            pltpu.make_async_remote_copy(
                src_ref=leaving.at[0], dst_ref=mirror.at[s],
                send_sem=back_sem.at[0], recv_sem=mirror_sem.at[s],
                device_id=at(side), device_id_type=pl.DeviceIdType.MESH).wait_recv()
            other = mirror[s]
            value += jnp.concatenate([other[:, :blk], other[:, blk:]], axis=0)
        out[:, s * blk:(s + 1) * blk] = value
    for copy in sends:
        copy.wait_send()


def body(partner_aux_tiles, row_aux_tiles, tile_partner, tile_count, density_blocks,
         density_cols, density_count):
    n = lax.axis_size("row")
    slots, blk, width = row_aux_tiles.shape
    dense = density_blocks.shape[0]
    window = 2 * REACH + 1
    span = width // CHUNKS
    vmem = pl.BlockSpec(memory_space=pltpu.VMEM)
    smem = pl.BlockSpec(memory_space=pltpu.SMEM)
    hbm = pl.BlockSpec(memory_space=pl.ANY)
    bf16 = jnp.bfloat16
    return pl.pallas_call(
        functools.partial(kernel, n),
        out_shape=jax.ShapeDtypeStruct((blk, window * blk), jnp.float32),
        in_specs=[hbm, hbm, smem, smem, hbm, smem, smem],
        out_specs=vmem,
        scratch_shapes=[
            pltpu.VMEM((slots, blk, width), bf16),
            pltpu.VMEM((slots, blk, width), bf16),
            pltpu.VMEM((dense, blk, blk), bf16),
            pltpu.VMEM((width, width), bf16),
            pltpu.VMEM((slots, blk, width), bf16),
            pltpu.VMEM((slots, blk, width), bf16),
            pltpu.VMEM((slots, 256, 256), bf16),
            pltpu.VMEM((CHUNKS, blk, span), bf16),
            pltpu.VMEM((10, CHUNKS, blk, span), bf16),
            pltpu.VMEM((window, blk, blk), jnp.float32),
            pltpu.VMEM((10, blk // 2, 2 * blk), jnp.float32),
            pltpu.VMEM((window, blk // 2, 2 * blk), jnp.float32),
            pltpu.SemaphoreType.DMA((3,)),
            pltpu.SemaphoreType.DMA((5, CHUNKS)),
            pltpu.SemaphoreType.DMA((5, CHUNKS)),
            pltpu.SemaphoreType.DMA((10, CHUNKS)),
            pltpu.SemaphoreType.DMA((10,)),
            pltpu.SemaphoreType.DMA((window,)),
        ],
        compiler_params=pltpu.CompilerParams(
            collective_id=0, has_side_effects=True, vmem_limit_bytes=60 * 2**20),
        cost_estimate=pl.CostEstimate(flops=2 * 10**9, bytes_accessed=3 * 2**20, transcendentals=0),
    )(row_aux_tiles, partner_aux_tiles, tile_partner, tile_count, density_blocks, density_cols,
      density_count)


def solution(mesh):
    in_specs = (
        P(("groups", "row"), None, None),
        P(("groups", "row"), None, None),
        P(("groups", "row")),
        P(("groups", "row")),
        P(("groups", "row"), None, None),
        P(("groups", "row")),
        P(("groups", "row")),
    )
    out_specs = P(("groups", "row"), None)
    return jax.shard_map(body, mesh=mesh, in_specs=in_specs, out_specs=out_specs, check_vma=False)
```

```python
import functools

import jax
import jax.numpy as jnp
from jax import lax
from jax.experimental import pallas as pl
from jax.experimental.pallas import tpu as pltpu
from jax.sharding import PartitionSpec as P

REACH = 5
CHUNKS = 2
N_T = (((1,), (1,)), ((), ()))


def kernel(n, row_hbm, pair_hbm, partner, count, density_hbm, cols, dense_count, out,
           row_v, pair_v, density, perm, row_p, pair_p, weights, mine, near, half, leaving, mirror,
           load_sem, send_sem, pass_sem, near_sem, back_sem, mirror_sem):
    slots, blk, width = row_v.shape
    dense = density.shape[0]
    aux = width // blk
    group = 256
    n_group = width // group
    per_chunk = n_group // CHUNKS
    span = width // CHUNKS

    me = lax.axis_index("row")
    core = lax.rem(me, 2)
    column = lax.rem(lax.div(me, 2), 2)
    side = 1 - 2 * core
    ahead = 1 - 2 * column
    inner = lax.rem(core + column, 2)

    def at(offset):
        return {"row": lax.rem(me + offset + n, n)}

    load_row = pltpu.make_async_copy(row_hbm, row_v, load_sem.at[0])
    load_pair = pltpu.make_async_copy(pair_hbm, pair_v, load_sem.at[1])
    load_density = pltpu.make_async_copy(density_hbm, density, load_sem.at[2])
    load_density.start()
    load_row.start()
    load_pair.start()
    barrier = pltpu.get_barrier_semaphore()
    for offset in range(-REACH, REACH + 1):
        if offset:
            pl.semaphore_signal(barrier, inc=1, device_id=at(offset),
                                device_id_type=pl.DeviceIdType.MESH)

    x = lax.broadcasted_iota(jnp.int32, (width, 128), 0)
    goes_to = lax.div(x, aux) + lax.rem(x, aux) * blk
    lane = lax.broadcasted_iota(jnp.int32, (width, 128), 1)
    for tile in range(width // 128):
        perm[:, tile * 128:(tile + 1) * 128] = jnp.where(
            goes_to == lane + tile * 128, 1.0, 0.0).astype(jnp.bfloat16)

    load_density.wait()
    live_tiles = count[0]
    live_dense = dense_count[0]
    zero = jnp.zeros((blk, blk), jnp.bfloat16)
    wide_zero = jnp.zeros((2 * blk, 2 * blk), jnp.bfloat16)
    for u in range(slots):
        index = jnp.int32(0)
        found = jnp.int32(0)
        for j in range(dense):
            hit = ((cols[j] == partner[u]) & (j < live_dense)).astype(jnp.int32)
            index += hit * j
            found += hit
        found *= (u < live_tiles).astype(jnp.int32)
        d = (density[index].astype(jnp.float32) * found.astype(jnp.float32)).astype(jnp.bfloat16)
        left = jnp.concatenate([d, zero], axis=1)
        right = jnp.concatenate([zero, d], axis=1)
        weights[u, 0:64, 0:128] = left
        weights[u, 64:128, 0:128] = right
        weights[u, 128:192, 128:256] = left
        weights[u, 192:256, 128:256] = right
        weights[u, 0:128, 128:256] = wide_zero
        weights[u, 128:256, 0:128] = wide_zero

    def reorder(source, target, g):
        flat = source[...].reshape(slots * blk, width)
        part = jnp.dot(flat, perm[:, g * group:(g + 1) * group],
                       preferred_element_type=jnp.float32)
        target[:, :, g * group:(g + 1) * group] = part.astype(jnp.bfloat16).reshape(
            slots, blk, group)

    sends = []

    def to_slot(source, slot, h, sem, offset):
        return pltpu.make_async_remote_copy(
            src_ref=source, dst_ref=near.at[slot, h], send_sem=sem, recv_sem=near_sem.at[slot, h],
            device_id=at(offset), device_id_type=pl.DeviceIdType.MESH)

    def put(source, slot, h, sem, offset):
        copy = to_slot(source, slot, h, sem, offset)
        copy.start()
        sends.append(copy)

    load_row.wait()
    for h in range(CHUNKS):
        for step in range(per_chunk):
            g = h * per_chunk + step
            reorder(row_v, row_p, g)
            total = jnp.zeros((blk, group), jnp.float32)
            for u in range(slots):
                total += lax.dot_general(row_p[u, :, g * group:(g + 1) * group], weights[u], N_T,
                                         preferred_element_type=jnp.float32)
            mine[h, :, step * group:(step + 1) * group] = total.astype(jnp.bfloat16)
        if h == 0:
            pl.semaphore_wait(barrier, 2 * REACH)
        for number, slot, offset in ((0, 1, -4 * ahead), (1, 2, 4 * ahead), (2, 0, 2 * ahead),
                                     (3, 4, side)):
            put(mine.at[h], slot, h, send_sem.at[number, h], offset)
        far = to_slot(mine.at[h], 9, h, send_sem.at[4, h], -5 * ahead)

        @pl.when(inner == 0)
        def _():
            far.start()

        sends.append(far)

    def arrived(slot, h):
        to_slot(mine.at[h], slot, h, send_sem.at[0, h], side).wait_recv()

    def pass_on(step):
        for slot, h in ((1, step), (2, step), (0, step), (3, step - 1)):
            if h < 0 or h >= CHUNKS:
                continue
            arrived(slot, h)
            if slot == 1:
                put(near.at[1, h], 3, h, pass_sem.at[4, h], 2 * ahead)
            if slot == 2:
                @pl.when(inner == 1)
                def _():
                    to_slot(near.at[2, h], 9, h, send_sem.at[4, h], ahead).start()
            put(near.at[slot, h], 5 + slot, h, pass_sem.at[slot, h], side)

    load_pair.wait()
    for g in range(n_group):
        reorder(pair_v, pair_p, g)
        if (g + 1) % per_chunk == 0:
            pass_on(g // per_chunk)

    where = [lax.rem(partner[t] - me + REACH + n, n) - REACH for t in range(slots)]

    def term(offset, block):
        index = jnp.int32(0)
        found = jnp.int32(0)
        for t in range(slots):
            hit = ((where[t] == offset) & (t < live_tiles)).astype(jnp.int32)
            index += hit * t
            found += hit
        total = jnp.zeros((blk, blk), jnp.float32)
        for h in range(CHUNKS):
            total += lax.dot_general(pair_p[index, :, h * span:(h + 1) * span], block(h), N_T,
                                     preferred_element_type=jnp.float32)
        return total * found.astype(jnp.float32)

    own = term(0, lambda h: mine[h])
    half[REACH] = own + own.T

    order = [(4, side), (0, 2 * ahead), (1, 4 * ahead), (2, -4 * ahead), (5, side + 2 * ahead),
             (3, -2 * ahead), (6, side + 4 * ahead), (7, side - 4 * ahead),
             (8, side - 2 * ahead), (9, -5 * side)]
    def settle(slot, offset):
        if slot >= 4:
            for h in range(CHUNKS):
                arrived(slot, h)
        value = term(offset, lambda h: near[slot, h])
        half[REACH + offset] = value
        turned = value.T
        leaving[slot] = jnp.concatenate([turned[:blk // 2], turned[blk // 2:]], axis=1)
        copy = pltpu.make_async_remote_copy(
            src_ref=leaving.at[slot], dst_ref=mirror.at[REACH - offset],
            send_sem=back_sem.at[slot], recv_sem=mirror_sem.at[REACH - offset],
            device_id=at(offset), device_id_type=pl.DeviceIdType.MESH)
        copy.start()
        sends.append(copy)

    for slot, offset in order[:2]:
        settle(slot, offset)
    pass_on(CHUNKS)
    for slot, offset in order[2:]:
        settle(slot, offset)

    for s in range(2 * REACH + 1):
        value = half[s]
        if s != REACH:
            pltpu.make_async_remote_copy(
                src_ref=leaving.at[0], dst_ref=mirror.at[s],
                send_sem=back_sem.at[0], recv_sem=mirror_sem.at[s],
                device_id=at(side), device_id_type=pl.DeviceIdType.MESH).wait_recv()
            other = mirror[s]
            value += jnp.concatenate([other[:, :blk], other[:, blk:]], axis=0)
        out[:, s * blk:(s + 1) * blk] = value
    for copy in sends:
        copy.wait_send()


def body(partner_aux_tiles, row_aux_tiles, tile_partner, tile_count, density_blocks,
         density_cols, density_count):
    n = lax.axis_size("row")
    slots, blk, width = row_aux_tiles.shape
    dense = density_blocks.shape[0]
    window = 2 * REACH + 1
    span = width // CHUNKS
    vmem = pl.BlockSpec(memory_space=pltpu.VMEM)
    smem = pl.BlockSpec(memory_space=pltpu.SMEM)
    hbm = pl.BlockSpec(memory_space=pl.ANY)
    bf16 = jnp.bfloat16
    return pl.pallas_call(
        functools.partial(kernel, n),
        out_shape=jax.ShapeDtypeStruct((blk, window * blk), jnp.float32),
        in_specs=[hbm, hbm, smem, smem, hbm, smem, smem],
        out_specs=vmem,
        scratch_shapes=[
            pltpu.VMEM((slots, blk, width), bf16),
            pltpu.VMEM((slots, blk, width), bf16),
            pltpu.VMEM((dense, blk, blk), bf16),
            pltpu.VMEM((width, width), bf16),
            pltpu.VMEM((slots, blk, width), bf16),
            pltpu.VMEM((slots, blk, width), bf16),
            pltpu.VMEM((slots, 256, 256), bf16),
            pltpu.VMEM((CHUNKS, blk, span), bf16),
            pltpu.VMEM((10, CHUNKS, blk, span), bf16),
            pltpu.VMEM((window, blk, blk), jnp.float32),
            pltpu.VMEM((10, blk // 2, 2 * blk), jnp.float32),
            pltpu.VMEM((window, blk // 2, 2 * blk), jnp.float32),
            pltpu.SemaphoreType.DMA((3,)),
            pltpu.SemaphoreType.DMA((5, CHUNKS)),
            pltpu.SemaphoreType.DMA((5, CHUNKS)),
            pltpu.SemaphoreType.DMA((10, CHUNKS)),
            pltpu.SemaphoreType.DMA((10,)),
            pltpu.SemaphoreType.DMA((window,)),
        ],
        compiler_params=pltpu.CompilerParams(
            collective_id=0, has_side_effects=True, vmem_limit_bytes=60 * 2**20),
        cost_estimate=pl.CostEstimate(flops=2 * 10**9, bytes_accessed=3 * 2**20, transcendentals=0),
    )(row_aux_tiles, partner_aux_tiles, tile_partner, tile_count, density_blocks, density_cols,
      density_count)


def solution(mesh):
    in_specs = (
        P(("groups", "row"), None, None),
        P(("groups", "row"), None, None),
        P(("groups", "row")),
        P(("groups", "row")),
        P(("groups", "row"), None, None),
        P(("groups", "row")),
        P(("groups", "row")),
    )
    out_specs = P(("groups", "row"), None)
    return jax.shard_map(body, mesh=mesh, in_specs=in_specs, out_specs=out_specs, check_vma=False)
```

```python
import functools

import jax
import jax.numpy as jnp
from jax import lax
from jax.experimental import pallas as pl
from jax.experimental.pallas import tpu as pltpu
from jax.sharding import PartitionSpec as P

REACH = 5
CHUNKS = 2
N_T = (((1,), (1,)), ((), ()))


def kernel(n, row_hbm, pair_hbm, partner, count, density_hbm, cols, dense_count, out,
           row_v, pair_v, density, perm, row_p, pair_p, weights, mine, near, first, half, leaving, mirror,
           load_sem, send_sem, pass_sem, near_sem, back_sem, mirror_sem):
    slots, blk, width = row_v.shape
    dense = density.shape[0]
    aux = width // blk
    group = 256
    n_group = width // group
    per_chunk = n_group // CHUNKS
    span = width // CHUNKS

    me = lax.axis_index("row")
    core = lax.rem(me, 2)
    column = lax.rem(lax.div(me, 2), 2)
    side = 1 - 2 * core
    ahead = 1 - 2 * column
    inner = lax.rem(core + column, 2)

    def at(offset):
        return {"row": lax.rem(me + offset + n, n)}

    load_row = pltpu.make_async_copy(row_hbm, row_v, load_sem.at[0])
    load_pair = pltpu.make_async_copy(pair_hbm, pair_v, load_sem.at[1])
    load_density = pltpu.make_async_copy(density_hbm, density, load_sem.at[2])
    load_density.start()
    load_row.start()
    load_pair.start()
    barrier = pltpu.get_barrier_semaphore()
    for offset in range(-REACH, REACH + 1):
        if offset:
            pl.semaphore_signal(barrier, inc=1, device_id=at(offset),
                                device_id_type=pl.DeviceIdType.MESH)

    x = lax.broadcasted_iota(jnp.int32, (width, 128), 0)
    goes_to = lax.div(x, aux) + lax.rem(x, aux) * blk
    lane = lax.broadcasted_iota(jnp.int32, (width, 128), 1)
    for tile in range(width // 128):
        perm[:, tile * 128:(tile + 1) * 128] = jnp.where(
            goes_to == lane + tile * 128, 1.0, 0.0).astype(jnp.bfloat16)

    load_density.wait()
    live_tiles = count[0]
    live_dense = dense_count[0]
    zero = jnp.zeros((blk, blk), jnp.bfloat16)
    wide_zero = jnp.zeros((2 * blk, 2 * blk), jnp.bfloat16)
    for u in range(slots):
        index = jnp.int32(0)
        found = jnp.int32(0)
        for j in range(dense):
            hit = ((cols[j] == partner[u]) & (j < live_dense)).astype(jnp.int32)
            index += hit * j
            found += hit
        found *= (u < live_tiles).astype(jnp.int32)
        d = (density[index].astype(jnp.float32) * found.astype(jnp.float32)).astype(jnp.bfloat16)
        left = jnp.concatenate([d, zero], axis=1)
        right = jnp.concatenate([zero, d], axis=1)
        weights[u, 0:64, 0:128] = left
        weights[u, 64:128, 0:128] = right
        weights[u, 128:192, 128:256] = left
        weights[u, 192:256, 128:256] = right
        weights[u, 0:128, 128:256] = wide_zero
        weights[u, 128:256, 0:128] = wide_zero

    def reorder(source, target, g):
        flat = source[...].reshape(slots * blk, width)
        part = jnp.dot(flat, perm[:, g * group:(g + 1) * group],
                       preferred_element_type=jnp.float32)
        target[:, :, g * group:(g + 1) * group] = part.astype(jnp.bfloat16).reshape(
            slots, blk, group)

    sends = []

    def to_slot(source, slot, h, sem, offset):
        return pltpu.make_async_remote_copy(
            src_ref=source, dst_ref=near.at[slot, h], send_sem=sem, recv_sem=near_sem.at[slot, h],
            device_id=at(offset), device_id_type=pl.DeviceIdType.MESH)

    def put(source, slot, h, sem, offset):
        copy = to_slot(source, slot, h, sem, offset)
        copy.start()
        sends.append(copy)

    load_row.wait()
    for h in range(CHUNKS):
        for step in range(per_chunk):
            g = h * per_chunk + step
            reorder(row_v, row_p, g)
            total = jnp.zeros((blk, group), jnp.float32)
            for u in range(slots):
                total += lax.dot_general(row_p[u, :, g * group:(g + 1) * group], weights[u], N_T,
                                         preferred_element_type=jnp.float32)
            mine[h, :, step * group:(step + 1) * group] = total.astype(jnp.bfloat16)
        if h == 0:
            pl.semaphore_wait(barrier, 2 * REACH)
        for number, slot, offset in ((0, 1, -4 * ahead), (1, 2, 4 * ahead), (2, 0, 2 * ahead),
                                     (3, 4, side)):
            put(mine.at[h], slot, h, send_sem.at[number, h], offset)
        far = to_slot(mine.at[h], 9, h, send_sem.at[4, h], -5 * ahead)

        @pl.when(inner == 0)
        def _():
            far.start()

        sends.append(far)

    def arrived(slot, h):
        to_slot(mine.at[h], slot, h, send_sem.at[0, h], side).wait_recv()

    def pass_on(step):
        for slot, h in ((1, step), (2, step), (0, step), (3, step - 1)):
            if h < 0 or h >= CHUNKS:
                continue
            arrived(slot, h)
            if slot == 1:
                put(near.at[1, h], 3, h, pass_sem.at[4, h], 2 * ahead)
            if slot == 2:
                @pl.when(inner == 1)
                def _():
                    to_slot(near.at[2, h], 9, h, send_sem.at[4, h], ahead).start()
            put(near.at[slot, h], 5 + slot, h, pass_sem.at[slot, h], side)

    load_pair.wait()
    for g in range(n_group):
        reorder(pair_v, pair_p, g)
        if (g + 1) % per_chunk == 0:
            pass_on(g // per_chunk)

    where = [lax.rem(partner[t] - me + REACH + n, n) - REACH for t in range(slots)]

    def chosen(offset):
        index = jnp.int32(0)
        found = jnp.int32(0)
        for t in range(slots):
            hit = ((where[t] == offset) & (t < live_tiles)).astype(jnp.int32)
            index += hit * t
            found += hit
        return index, found.astype(jnp.float32)

    def term(index, h, block):
        return lax.dot_general(pair_p[index, :, h * span:(h + 1) * span], block, N_T,
                               preferred_element_type=jnp.float32)

    index, found = chosen(0)
    own = sum(term(index, h, mine[h]) for h in range(CHUNKS)) * found
    half[REACH] = own + own.T

    order = [(4, side), (0, 2 * ahead), (1, 4 * ahead), (2, -4 * ahead), (5, side + 2 * ahead),
             (3, -2 * ahead), (6, side + 4 * ahead), (7, side - 4 * ahead),
             (8, side - 2 * ahead), (9, -5 * side)]
    picks = {slot: chosen(offset) for slot, offset in order}
    started = []

    def begin(slot):
        if slot >= 4:
            for h in range(CHUNKS - 1):
                arrived(slot, h)
        index, _ = picks[slot]
        first[slot] = sum(term(index, h, near[slot, h]) for h in range(CHUNKS - 1))
        started.append(slot)

    def settle(slot, offset):
        if slot not in started:
            begin(slot)
        if slot >= 4:
            arrived(slot, CHUNKS - 1)
        index, found = picks[slot]
        value = (first[slot] + term(index, CHUNKS - 1, near[slot, CHUNKS - 1])) * found
        half[REACH + offset] = value
        turned = value.T
        leaving[slot] = jnp.concatenate([turned[:blk // 2], turned[blk // 2:]], axis=1)
        copy = pltpu.make_async_remote_copy(
            src_ref=leaving.at[slot], dst_ref=mirror.at[REACH - offset],
            send_sem=back_sem.at[slot], recv_sem=mirror_sem.at[REACH - offset],
            device_id=at(offset), device_id_type=pl.DeviceIdType.MESH)
        copy.start()
        sends.append(copy)

    for slot, offset in order[:2]:
        settle(slot, offset)
    for slot in (1, 2, 3, 6, 7, 9):
        begin(slot)
    pass_on(CHUNKS)
    for slot, offset in order[2:]:
        settle(slot, offset)

    for s in sorted(range(2 * REACH + 1), key=lambda s: abs(s - REACH)):
        value = half[s]
        if s != REACH:
            pltpu.make_async_remote_copy(
                src_ref=leaving.at[0], dst_ref=mirror.at[s],
                send_sem=back_sem.at[0], recv_sem=mirror_sem.at[s],
                device_id=at(side), device_id_type=pl.DeviceIdType.MESH).wait_recv()
            other = mirror[s]
            value += jnp.concatenate([other[:, :blk], other[:, blk:]], axis=0)
        out[:, s * blk:(s + 1) * blk] = value
    for copy in sends:
        copy.wait_send()


def body(partner_aux_tiles, row_aux_tiles, tile_partner, tile_count, density_blocks,
         density_cols, density_count):
    n = lax.axis_size("row")
    slots, blk, width = row_aux_tiles.shape
    dense = density_blocks.shape[0]
    window = 2 * REACH + 1
    span = width // CHUNKS
    vmem = pl.BlockSpec(memory_space=pltpu.VMEM)
    smem = pl.BlockSpec(memory_space=pltpu.SMEM)
    hbm = pl.BlockSpec(memory_space=pl.ANY)
    bf16 = jnp.bfloat16
    return pl.pallas_call(
        functools.partial(kernel, n),
        out_shape=jax.ShapeDtypeStruct((blk, window * blk), jnp.float32),
        in_specs=[hbm, hbm, smem, smem, hbm, smem, smem],
        out_specs=vmem,
        scratch_shapes=[
            pltpu.VMEM((slots, blk, width), bf16),
            pltpu.VMEM((slots, blk, width), bf16),
            pltpu.VMEM((dense, blk, blk), bf16),
            pltpu.VMEM((width, width), bf16),
            pltpu.VMEM((slots, blk, width), bf16),
            pltpu.VMEM((slots, blk, width), bf16),
            pltpu.VMEM((slots, 256, 256), bf16),
            pltpu.VMEM((CHUNKS, blk, span), bf16),
            pltpu.VMEM((10, CHUNKS, blk, span), bf16),
            pltpu.VMEM((10, blk, blk), jnp.float32),
            pltpu.VMEM((window, blk, blk), jnp.float32),
            pltpu.VMEM((10, blk // 2, 2 * blk), jnp.float32),
            pltpu.VMEM((window, blk // 2, 2 * blk), jnp.float32),
            pltpu.SemaphoreType.DMA((3,)),
            pltpu.SemaphoreType.DMA((5, CHUNKS)),
            pltpu.SemaphoreType.DMA((5, CHUNKS)),
            pltpu.SemaphoreType.DMA((10, CHUNKS)),
            pltpu.SemaphoreType.DMA((10,)),
            pltpu.SemaphoreType.DMA((window,)),
        ],
        compiler_params=pltpu.CompilerParams(
            collective_id=0, has_side_effects=True, vmem_limit_bytes=60 * 2**20),
        cost_estimate=pl.CostEstimate(flops=2 * 10**9, bytes_accessed=3 * 2**20, transcendentals=0),
    )(row_aux_tiles, partner_aux_tiles, tile_partner, tile_count, density_blocks, density_cols,
      density_count)


def solution(mesh):
    in_specs = (
        P(("groups", "row"), None, None),
        P(("groups", "row"), None, None),
        P(("groups", "row")),
        P(("groups", "row")),
        P(("groups", "row"), None, None),
        P(("groups", "row")),
        P(("groups", "row")),
    )
    out_specs = P(("groups", "row"), None)
    return jax.shard_map(body, mesh=mesh, in_specs=in_specs, out_specs=out_specs, check_vma=False)
```
